32 devices in a mesh: node: 8 (over y, x, core), local: 4 (over z).
Axes of the slice: x: 2, y: 2, z: 4, core: 2. Of those that a mesh axis runs over, the one named last changes fastest.
Arguments:
- quantized: bfloat16 [512, 3584], P(('node', 'local')), may hold values from -6 to 6
- scales: bfloat16 [512, 28], P(('node', 'local')), may hold values from 0.29882812 to 3
- expert_ids: int32 [512, 8], P(('node', 'local')), may hold values from 0 to 31, as said below
- node_choice: int32 [512, 4], P(('node', 'local')), may hold values from 0 to 7, as said below
- gate_weights: bfloat16 [512, 8], P(('node', 'local')), may hold values from 0.099609375 to 1
- w_gate: bfloat16 [32, 3584, 1024], P(('node', 'local')), may hold values from -0.09375 to 0.09375
- w_up: bfloat16 [32, 3584, 1024], P(('node', 'local')), may hold values from -0.09375 to 0.09375
- w_down: bfloat16 [32, 1024, 3584], P(('node', 'local')), may hold values from -0.1875 to 0.1875
Outputs:
- mixed: bfloat16 [512, 3584], P(('node', 'local'))
The draws below stay inside these ranges and needn't reach their ends.
Inputs may be any that keep to these rules, and one draw needn't show every extreme that they name: `expert_ids`: each token names 8 distinct experts, all on nodes listed for it in node_choice (expert e is on node e // 4), and each listed node holds at least one of them. In every draw one expert is named exactly 8 times by the tokens of every device. `node_choice`: each token lists 4 distinct nodes. The tokens of one device (aligned blocks of 16 rows) list every node exactly 8 times, so they name each expert at most 8 times.
All inputs are finite; a program needn't handle non-finite values.
Results may differ from the reference program's by a relative error of at most 0.012.
Values may be sent and summed in bfloat16 or wider, within the bound.
A program may use at most 128 MiB of HBM per device.

```python
import math
import jax
import jax.numpy as jnp
from jax import lax

D = 3584
FF = 1024
TOPK = 8
NODE_LIMIT = 4
TOK_DEV = 16
EXPERTS = 32
TOKENS = 512
CAP = 8
N_NODE = 8
N_LOCAL = 4


def route_tables(key):
    devices = N_NODE * N_LOCAL
    subkeys = jax.random.split(key, 7)
    favorite = jax.random.randint(subkeys[0], (), 0, devices)
    hot_node = favorite // N_LOCAL
    hot_local = favorite % N_LOCAL
    offsets = jax.vmap(lambda subkey: jax.random.permutation(subkey, N_NODE)[:NODE_LIMIT])(jax.random.split(subkeys[1], devices))
    shuffled = jax.vmap(lambda subkey: jax.random.permutation(subkey, TOK_DEV))(jax.random.split(subkeys[2], devices))
    residue = shuffled % N_NODE
    chosen = (offsets[:, None, :] + residue[:, :, None]) % N_NODE
    raised = jax.random.randint(subkeys[3], (devices, TOK_DEV, 1), 0, NODE_LIMIT)
    lowered = (raised + jax.random.randint(subkeys[4], (devices, TOK_DEV, 1), 1, NODE_LIMIT)) % NODE_LIMIT
    switch = jax.random.randint(subkeys[5], (devices, TOK_DEV, 1), 0, 2)
    columns = jnp.arange(NODE_LIMIT, dtype=jnp.int32)[None, None, :]
    counts = 2 + switch * (columns == raised).astype(jnp.int32) - switch * (columns == lowered).astype(jnp.int32)
    local_index = jnp.arange(N_LOCAL, dtype=jnp.int32)
    scores = jax.random.randint(subkeys[6], (devices, TOK_DEV, NODE_LIMIT, N_LOCAL), 0, 1 << 20) * N_LOCAL + local_index
    favored = (chosen[..., None] == hot_node) & (local_index == hot_local)
    scores = jnp.where(favored, -1, scores)
    ranking = jnp.argsort(scores, axis=-1, stable=True).astype(jnp.int32)
    candidate = (chosen[..., None] * N_LOCAL + ranking).reshape(devices, TOK_DEV, NODE_LIMIT * N_LOCAL)
    usable = (local_index < counts[..., None]).reshape(devices, TOK_DEV, NODE_LIMIT * N_LOCAL)
    position = jnp.cumsum(usable.astype(jnp.int32), axis=-1) - 1
    pick_index = jnp.arange(TOPK, dtype=jnp.int32)
    selected = usable[..., None] & (position[..., None] == pick_index)
    expert_ids = jnp.sum(jnp.where(selected, candidate[..., None], 0), axis=-2)
    return (expert_ids.reshape(devices * TOK_DEV, TOPK).astype(jnp.int32), chosen.reshape(devices * TOK_DEV, NODE_LIMIT).astype(jnp.int32))


def draw_expert_ids(key, part):
    return route_tables(jax.random.fold_in(key, 11))[0]


def draw_node_choice(key, part):
    return route_tables(jax.random.fold_in(key, 11))[1]


def block_levels(rng, shape, cuts, low, largest):
    level, own = 1.0, jax.random.fold_in(rng, 6)
    for dim, parts in cuts:
        draws = jnp.exp(jax.random.uniform(jax.random.fold_in(own, dim), (parts,), jnp.float32, low / len(cuts), largest / len(cuts)))
        level = level * jnp.repeat(draws, shape[dim] // parts).reshape([-1 if axis == dim else 1 for axis in range(len(shape))])
    return level


def scatter_about(stream_key, shape, spread, bound, cuts=(), kind=jnp.bfloat16):
    values = jax.random.normal(stream_key, shape, jnp.float32) * spread
    if len(cuts) > 0:
        values = block_levels(stream_key, shape, cuts, -0.22, 0.18) * values
    return jnp.clip(values, min=-bound, max=bound).astype(kind)


def setup_inputs(seed: int = 0) -> dict:
    streams_of = jax.random.split(jax.random.key(seed), 9)
    quantized = scatter_about(streams_of[0], (TOKENS, D), 1.0, 6.0, ((0, 32),))
    scales = jnp.clip(jnp.exp(math.log(3.0) - 2.306499 * jax.random.uniform(streams_of[1], (TOKENS, D // 128), jnp.float32) ** block_levels(streams_of[1], (TOKENS, D // 128), ((0, 32),), -0.2, 0.2)), 0.29882812, 3.0).astype(jnp.bfloat16)
    expert_ids = draw_expert_ids(jax.random.fold_in(streams_of[8], 71), 0)
    node_choice = draw_node_choice(jax.random.fold_in(streams_of[8], 71), 0)
    gate_weights = jnp.clip(jnp.exp(math.log(1.0) - 2.306499 * jax.random.uniform(streams_of[4], (TOKENS, TOPK), jnp.float32) ** block_levels(streams_of[4], (TOKENS, TOPK), ((0, 32),), -0.2, 0.2)), 0.099609375, 1.0).astype(jnp.bfloat16)
    w_gate = scatter_about(streams_of[5], (EXPERTS, D, FF), D ** -0.5, 0.09375, ((0, 32),))
    w_up = scatter_about(streams_of[6], (EXPERTS, D, FF), D ** -0.5, 0.09375, ((0, 32),))
    w_down = scatter_about(streams_of[7], (EXPERTS, FF, D), FF ** -0.5, 0.1875, ((0, 32),))
    return {"quantized": quantized, "scales": scales, "expert_ids": expert_ids, "node_choice": node_choice, "gate_weights": gate_weights, "w_gate": w_gate, "w_up": w_up, "w_down": w_down}


def expert_apply(quant_rows, scale_rows, gate_proj, up_proj, down_proj):
    row_count = quant_rows.shape[0]
    blocks = scale_rows.shape[1]
    widened = quant_rows.reshape(row_count, blocks, -1).astype(jnp.float32) * scale_rows.astype(jnp.float32)[:, :, None]
    inputs = widened.reshape(row_count, -1).astype(jnp.bfloat16)
    gate_act = jnp.dot(inputs, gate_proj, preferred_element_type=jnp.float32)
    up_act = jnp.dot(inputs, up_proj, preferred_element_type=jnp.float32)
    hidden = (jax.nn.silu(gate_act) * up_act).astype(jnp.bfloat16)
    return jnp.dot(hidden, down_proj, preferred_element_type=jnp.float32).astype(jnp.bfloat16)


def reference(quantized, scales, expert_ids, node_choice, gate_weights, w_gate, w_up, w_down):
    slot_span = N_NODE * N_LOCAL * CAP
    pair_total = TOKENS * NODE_LIMIT
    token_index = jnp.arange(TOKENS, dtype=jnp.int32)
    choice_index = jnp.arange(NODE_LIMIT, dtype=jnp.int32)
    weights = gate_weights.astype(jnp.float32)

    def one_expert(accum_rows, expert):
        hit_mask = expert_ids == expert
        named_mask = jnp.any(hit_mask, axis=1)
        ranking = jnp.cumsum(named_mask.astype(jnp.int32)) - 1
        spot_index = jnp.where(named_mask, ranking, slot_span).astype(jnp.int32)
        gathered = jnp.zeros((slot_span,), jnp.int32).at[spot_index].set(token_index, mode="drop")
        filled = jnp.arange(slot_span, dtype=jnp.int32) < jnp.sum(named_mask.astype(jnp.int32))
        result = expert_apply(quantized[gathered], scales[gathered], w_gate[expert], w_up[expert], w_down[expert])
        gate_value = jnp.sum(jnp.where(hit_mask, weights, 0.0), axis=1)
        node_match = node_choice == expert // N_LOCAL
        listed = jnp.any(node_match, axis=1)
        home_column = jnp.sum(jnp.where(node_match, choice_index, 0), axis=1).astype(jnp.int32)
        flat_target = token_index * NODE_LIMIT + home_column
        keep = filled & listed[gathered]
        destination = jnp.where(keep, flat_target[gathered], pair_total).astype(jnp.int32)
        weighted = (gate_value[gathered][:, None] * result.astype(jnp.float32)).astype(jnp.bfloat16)
        contrib = lax.optimization_barrier(weighted).astype(jnp.float32)
        return accum_rows.at[destination].add(contrib, mode="drop"), None

    initial = jnp.zeros((pair_total, D), jnp.float32)
    summed, unused = lax.scan(one_expert, initial, jnp.arange(EXPERTS, dtype=jnp.int32))
    partial_value = summed.reshape(TOKENS, NODE_LIMIT, D).astype(jnp.bfloat16)
    return jnp.sum(partial_value.astype(jnp.float32), axis=1).astype(jnp.bfloat16)
```

```python
import functools
import jax
import jax.numpy as jnp
from jax import lax
from jax.experimental import pallas as pl
from jax.experimental.pallas import tpu as pltpu
from jax.sharding import PartitionSpec as P

MESH = pl.DeviceIdType.MESH
LANES = 128
F32 = jnp.float32
BF16 = jnp.bfloat16


def round_up(value, step):
    return (value + step - 1) // step * step


def kernel(
    n_node, n_local, cap, parts,
    q_ref, scale_ref, ids_ref, choice_ref, gate_ref, wg_hbm, wu_hbm, wd_hbm,
    out_ref,
    wg, wu, wd, xz, packed, rows, inputs, hidden, result, back, zpart, zback,
    w_sem, z_send, z_recv, n_send, n_recv, r_send, r_recv, t_send, t_recv,
):
    me_n = lax.axis_index("node")
    me_l = lax.axis_index("local")
    tok, width = q_ref.shape
    slots = n_node * cap
    total = n_local * slots
    exp_w = rows.shape[3] - width
    part_w = width // parts
    ff = wg.shape[1]

    def node_at(step):
        return lax.rem(me_n + step, n_node)

    def local_at(step):
        return lax.rem(me_l + step, n_local)

    weight_copies = [
        pltpu.make_async_copy(src, dst, w_sem.at[i])
        for i, (src, dst) in enumerate(((wg_hbm, wg), (wu_hbm, wu), (wd_hbm, wd)))
    ]
    barrier = pltpu.get_barrier_semaphore()
    for step in range(1, n_node):
        pl.semaphore_signal(barrier, inc=1, device_id=(node_at(step), me_l), device_id_type=MESH)
    for step in range(1, n_local):
        pl.semaphore_signal(barrier, inc=1, device_id=(me_n, local_at(step)), device_id_type=MESH)
    for copy in weight_copies:
        copy.start()

    scale = scale_ref[...].astype(F32)
    block = width // scale.shape[1]
    for b in range(scale.shape[1]):
        cols = pl.ds(b * block, block)
        xz[me_l, :, cols] = (q_ref[:, cols].astype(F32) * scale[:, b : b + 1]).astype(BF16)
    ids = ids_ref[...]
    gate = gate_ref[...].astype(F32)
    expert_col = lax.broadcasted_iota(jnp.int32, (tok, exp_w), 1)
    weight = jnp.zeros((tok, exp_w), F32)
    for k in range(ids.shape[1]):
        weight = weight + jnp.where(ids[:, k : k + 1] == expert_col, gate[:, k : k + 1], 0.0)
    xz[me_l, :, pl.ds(width, exp_w)] = weight.astype(BF16)
    place_w = xz.shape[2] - width - exp_w
    column = lax.broadcasted_iota(jnp.int32, (tok, place_w), 1)
    node_col = lax.div(column, jnp.int32(cap))
    slot_col = lax.rem(column, jnp.int32(cap))
    choice = choice_ref[...]
    named = jnp.zeros((tok, place_w), F32)
    for j in range(choice.shape[1]):
        named = named + jnp.where(choice[:, j : j + 1] == node_col, 1.0, 0.0)
    before = jnp.where(
        lax.broadcasted_iota(jnp.int32, (tok, tok), 1) < lax.broadcasted_iota(jnp.int32, (tok, tok), 0), 1.0, 0.0
    )
    rank = jnp.dot(before.astype(BF16), named.astype(BF16), preferred_element_type=F32)
    place = jnp.where(rank == slot_col.astype(F32), named, 0.0)
    xz[me_l, :, pl.ds(width + exp_w, place_w)] = place.astype(BF16)

    pl.semaphore_wait(barrier, n_node + n_local - 2)

    def z_copy(step):
        return pltpu.make_async_remote_copy(
            src_ref=xz.at[me_l], dst_ref=xz.at[me_l],
            send_sem=z_send.at[step], recv_sem=z_recv.at[step],
            device_id=(me_n, local_at(step)), device_id_type=MESH,
        )

    for step in range(1, n_local):
        z_copy(step).start()

    def n_copy(source, step):
        return pltpu.make_async_remote_copy(
            src_ref=packed.at[source, node_at(step)], dst_ref=rows.at[source, me_n],
            send_sem=n_send.at[source, step], recv_sem=n_recv.at[source, step],
            device_id=(node_at(step), me_l), device_id_type=MESH,
        )

    def pack(source):
        picks = jnp.transpose(xz[source, :, pl.ds(width + exp_w, place_w)].astype(F32))[:slots].astype(BF16)
        value = jnp.dot(picks, xz[source, :, pl.ds(0, width + exp_w)], preferred_element_type=F32)
        packed[source] = value.reshape(n_node, cap, width + exp_w).astype(BF16)

        @pl.loop(1, n_node)
        def _(step):
            n_copy(source, step).start()

        rows[source, me_n] = packed[source, me_n]

    pack(me_l)

    @pl.loop(1, n_local)
    def _(step):
        z_copy(step).wait_recv()
        pack(lax.rem(me_l - step + n_local, n_local))

    @pl.loop(0, n_local)
    def _(source):
        @pl.loop(1, n_node)
        def _(step):
            n_copy(source, step).wait_recv()

    inputs[...] = rows[:, :, :, :width].astype(F32).reshape(total, width).astype(BF16)
    weights = rows[:, :, :, width:].astype(F32).reshape(total, exp_w)
    mine = lax.broadcasted_iota(jnp.int32, (total, exp_w), 1) == me_n * n_local + me_l
    row_weight = jnp.sum(jnp.where(mine, weights, 0.0), axis=1, keepdims=True)
    weight_copies[0].wait()
    weight_copies[1].wait()
    tile = 256

    @pl.loop(0, ff // tile)
    def _(i):
        cols = pl.ds(pl.multiple_of(i * tile, tile), tile)
        g = jnp.dot(inputs[...], wg[:, cols], preferred_element_type=F32)
        u = jnp.dot(inputs[...], wu[:, cols], preferred_element_type=F32)
        hidden[:, cols] = (g / (1.0 + jnp.exp(-g)) * u).astype(BF16)

    weight_copies[2].wait()

    def r_copy(h, step):
        return pltpu.make_async_remote_copy(
            src_ref=result.at[h, :, node_at(step)], dst_ref=back.at[h, :, me_n],
            send_sem=r_send.at[h, step], recv_sem=r_recv.at[h, step],
            device_id=(node_at(step), me_l), device_id_type=MESH,
        )

    @pl.loop(0, parts)
    def _(h):
        cols = pl.ds(pl.multiple_of(h * part_w, LANES), part_w)
        y = jnp.dot(hidden[...], wd[:, cols], preferred_element_type=F32)
        y = row_weight * y.astype(BF16).astype(F32)
        result[h] = y.reshape(n_local, n_node, cap, part_w).astype(BF16)

        @pl.loop(1, n_node)
        def _(step):
            r_copy(h, step).start()

        back[h, :, me_n] = result[h, :, me_n]

    def t_copy(h, step):
        return pltpu.make_async_remote_copy(
            src_ref=zpart.at[h, step], dst_ref=zback.at[h, step],
            send_sem=t_send.at[h, step], recv_sem=t_recv.at[h, step],
            device_id=(me_n, local_at(step)), device_id_type=MESH,
        )

    @pl.loop(0, parts)
    def _(h):
        @pl.loop(1, n_node)
        def _(step):
            r_copy(h, step).wait_recv()

        def gathered(source):
            spread = xz[source, :, pl.ds(width + exp_w, place_w)][:, :slots]
            found = back[h, source].astype(F32).reshape(slots, part_w).astype(BF16)
            return jnp.dot(spread, found, preferred_element_type=F32).astype(BF16)

        @pl.loop(1, n_local)
        def _(step):
            zpart[h, step] = gathered(local_at(step))
            t_copy(h, step).start()

        zback[h, 0] = gathered(me_l)

    for h in range(parts):
        @pl.loop(1, n_local)
        def _(step):
            t_copy(h, step).wait_recv()

        out_ref[:, pl.ds(h * part_w, part_w)] = jnp.sum(zback[h].astype(F32), axis=0).astype(BF16)

    @pl.loop(1, n_local)
    def _(step):
        z_copy(step).wait_send()

    @pl.loop(0, n_local)
    def _(source):
        @pl.loop(1, n_node)
        def _(step):
            n_copy(source, step).wait_send()

    @pl.loop(0, parts)
    def _(h):
        @pl.loop(1, n_node)
        def _(step):
            r_copy(h, step).wait_send()

        @pl.loop(1, n_local)
        def _(step):
            t_copy(h, step).wait_send()


def shards(quantized, scales, expert_ids, node_choice, gate_weights, w_gate, w_up, w_down):
    n_node = lax.axis_size("node")
    n_local = lax.axis_size("local")
    tok, width = quantized.shape
    ff = w_gate.shape[2]
    cap = node_choice.shape[1] * tok // n_node
    slots = n_node * cap
    total = n_local * slots
    parts = 4
    part_w = width // parts
    exp_w = round_up(n_node * n_local, LANES)
    place_w = round_up(slots, LANES)
    dma = pltpu.SemaphoreType.DMA
    vmem = pl.BlockSpec(memory_space=pltpu.VMEM)
    return pl.pallas_call(
        functools.partial(kernel, n_node, n_local, cap, parts),
        out_shape=jax.ShapeDtypeStruct((tok, width), BF16),
        in_specs=[vmem] * 5 + [pl.BlockSpec(memory_space=pl.ANY)] * 3,
        out_specs=vmem,
        scratch_shapes=[
            pltpu.VMEM((width, ff), BF16),
            pltpu.VMEM((width, ff), BF16),
            pltpu.VMEM((ff, width), BF16),
            pltpu.VMEM((n_local, tok, width + exp_w + place_w), BF16),
            pltpu.VMEM((n_local, n_node, cap, width + exp_w), BF16),
            pltpu.VMEM((n_local, n_node, cap, width + exp_w), BF16),
            pltpu.VMEM((total, width), BF16),
            pltpu.VMEM((total, ff), BF16),
            pltpu.VMEM((parts, n_local, n_node, cap, part_w), BF16),
            pltpu.VMEM((parts, n_local, n_node, cap, part_w), BF16),
            pltpu.VMEM((parts, n_local, tok, part_w), BF16),
            pltpu.VMEM((parts, n_local, tok, part_w), BF16),
            dma((3,)),
            dma((n_local,)), dma((n_local,)),
            dma((n_local, n_node)), dma((n_local, n_node)),
            dma((parts, n_node)), dma((parts, n_node)),
            dma((parts, n_local)), dma((parts, n_local)),
        ],
        compiler_params=pltpu.CompilerParams(
            collective_id=0, has_side_effects=True, vmem_limit_bytes=60 * 1024 * 1024
        ),
    )(
        quantized, scales, expert_ids, node_choice, gate_weights, w_gate[0], w_up[0], w_down[0]
    )


def solution(mesh):
    rows = P(("node", "local"), None)
    mats = P(("node", "local"), None, None)
    return jax.shard_map(
        shards,
        mesh=mesh,
        in_specs=(rows,) * 5 + (mats,) * 3,
        out_specs=rows,
        check_vma=False,
    )
```
